32 devices in a mesh: occ: 4 (over y, x), vir: 4 (over z), rep: 2 (over core).
Axes of the slice: x: 2, y: 2, z: 4, core: 2. Of those that a mesh axis runs over, the one named last changes fastest.
Arguments:
- amplitudes: bfloat16 [2048, 4096], P('occ', 'vir'), may hold values from -6 to 6
- integrals: bfloat16 [8, 24, 512, 512], P('vir', 'rep'), may hold values from -0.0546875 to 0.0546875
- cd_tiles: int32 [8, 24], P('vir', 'rep'), may hold values from 0 to 7, as said below
- occ_energy: float32 [2048], P('occ'), may hold values from -2 to -0.5
- pair_energy: float32 [4096], P('vir'), may hold values from 0.5 to 3
Outputs:
- resid: bfloat16 [2048, 4096], P(('occ', 'rep'), 'vir')
The draws below stay inside these ranges and needn't reach their ends.
Inputs may be any that keep to these rules, and one draw needn't show every extreme that they name: `cd_tiles`: every tile is named by some entry; a tile may be named more than once in a row.
All inputs are finite; a program needn't handle non-finite values.
Results may differ from the reference program's by a relative error of at most 0.007.
Values may be sent and summed in bfloat16 or wider, within the bound.
No kernel may reach another device: no remote copies, remote signals or barrier semaphores. Data moves between devices by JAX's collectives and lax.ppermute only.
A program may use at most 192 MiB of HBM per device.

```python
import jax
import jax.numpy as jnp
from jax import lax

PW = 512
NVT = 8
NV = 4096
NNZ = 24
OP = 2048


def draw_cd_tiles(key, part):
    key = jax.random.fold_in(key, 7)
    first_key, rest_key = jax.random.split(key)
    first = jax.random.permutation(first_key, NVT).astype(jnp.int32)
    others = jax.random.randint(rest_key, (NVT, NNZ - 1), 0, NVT).astype(jnp.int32)
    return jnp.concatenate([first[:, None], others], axis=1)


def steps_of(rng, extent, cuts, least, high):
    factor_of, own = 1.0, jax.random.fold_in(rng, 6)
    for axis_at, parts in cuts:
        draws = jnp.exp(jax.random.uniform(jax.random.fold_in(own, axis_at), (parts,), jnp.float32, least / len(cuts), high / len(cuts)))
        factor_of = factor_of * jnp.repeat(draws, extent[axis_at] // parts).reshape([-1 if axis == axis_at else 1 for axis in range(len(extent))])
    return factor_of


def gaussian(key, shape, width, reach, pieces=(), held_as=jnp.bfloat16):
    drawn = width * jax.random.normal(key, shape, jnp.float32)
    if pieces:
        drawn = drawn * steps_of(key, shape, pieces, -0.22, 0.18)
    return jnp.clip(drawn, -reach, reach).astype(held_as)


def setup_inputs(seed: int = 0) -> dict:
    key_of = jax.random.split(jax.random.key(seed), 6)
    return {
        "amplitudes": gaussian(key_of[0], (OP, NV), 1.0, 6.0, ((0, 4), (1, 4))),
        "integrals": gaussian(key_of[1], (NVT, NNZ, PW, PW), (NNZ * PW) ** -0.5, 0.0546875, ((0, 4), (1, 2))),
        "cd_tiles": draw_cd_tiles(jax.random.fold_in(key_of[5], 71), 0),
        "occ_energy": jnp.clip(-2.0 + 1.5 * jax.random.uniform(key_of[3], (OP,), jnp.float32) ** steps_of(key_of[3], (OP,), ((0, 4),), -0.2, 0.2), -2.0, -0.5),
        "pair_energy": jnp.clip(0.5 + 2.5 * jax.random.uniform(key_of[4], (NV,), jnp.float32) ** steps_of(key_of[4], (NV,), ((0, 4),), -0.2, 0.2), 0.5, 3.0),
    }


def reference(amplitudes, integrals, cd_tiles, occ_energy, pair_energy):
    row_count = amplitudes.shape[0]
    tile_view = amplitudes.reshape(row_count, NVT, PW)

    def one_tile(pair_args):
        blocks, chosen = pair_args
        picked = jnp.take(tile_view, chosen.astype(jnp.int32), axis=1).astype(jnp.float32)
        return jnp.einsum("rkp,kpq->rq", picked, blocks.astype(jnp.float32))

    ladder = lax.map(one_tile, (integrals, cd_tiles))
    ladder = jnp.transpose(ladder, (1, 0, 2)).reshape(row_count, NVT * PW)
    energy_gap = pair_energy[None, :] - occ_energy[:, None]
    return (ladder + energy_gap * amplitudes.astype(jnp.float32)).astype(jnp.bfloat16)
```

```python
import functools

import jax
import jax.numpy as jnp
from jax import lax
from jax.experimental import pallas as pl
from jax.experimental.pallas import tpu as pltpu
from jax.sharding import PartitionSpec as P

MIB = 1024 * 1024


def ladder_tiles(amp_rows, blocks, chosen, tile_width):
    row_count = amp_rows.shape[0]
    tile_view = amp_rows.reshape(row_count, -1, tile_width)
    picked = jnp.take(tile_view, chosen.reshape(-1), axis=1)
    picked = picked.reshape(row_count, chosen.shape[0], chosen.shape[1], tile_width)
    result = jnp.einsum("rakp,akpq->raq", picked, blocks, preferred_element_type=jnp.float32)
    return result.reshape(row_count, -1)


def sparse_local(amplitudes, integrals, cd_tiles, occ_energy, pair_energy):
    tile_width = integrals.shape[2]
    own_rows = amplitudes.shape[0]
    rep_rows = own_rows // lax.axis_size("rep")
    rep_index = lax.axis_index("rep")
    own_amps = lax.dynamic_slice_in_dim(amplitudes, rep_index * rep_rows, rep_rows, 0)
    whole = lax.all_gather(amplitudes, "vir", axis=1, tiled=True)
    partial_value = ladder_tiles(whole, integrals, cd_tiles, tile_width)
    sums = lax.psum_scatter(
        partial_value.astype(jnp.bfloat16), "rep", scatter_dimension=0, tiled=True
    ).astype(jnp.float32)
    own_occ = lax.dynamic_slice_in_dim(occ_energy, rep_index * rep_rows, rep_rows, 0)
    energy_gap = pair_energy[None, :] - own_occ[:, None]
    return (sums + energy_gap * own_amps.astype(jnp.float32)).astype(jnp.bfloat16)


ARRIVAL = ((0, 1, 2, 3), (1, 0, 2, 3), (2, 3, 1, 0), (3, 2, 1, 0))
PIECES = 2
STEP = 128
MOST = 4


def arrival_of(vir_index, place):
    chunk = jnp.int32(0)
    for index, chunks in enumerate(ARRIVAL):
        chunk = jnp.where(vir_index == index, chunks[place], chunk)
    return chunk


def list_entries(vir_index, sources, count_ref, entry_ref, per, n_held):
    n_place = len(ARRIVAL[0])
    places = [jnp.int32(0)] * n_place
    for place in range(n_place):
        for chunk in range(n_place):
            places[chunk] = jnp.where(arrival_of(vir_index, place) == chunk, place, places[chunk])

    @pl.loop(0, count_ref.shape[0])
    def _(s):
        count_ref[s] = 0

    for chosen_ref, a, i, taken, first in sources:
        for k in taken:
            tile = chosen_ref[a, k]
            chunk = lax.div(tile, per)
            place = places[0]
            for other in range(1, n_place):
                place = jnp.where(chunk == other, places[other], place)
            s = (i * n_place + place) * per + lax.rem(tile, per)
            at = count_ref[s]
            entry_ref[s * n_held + at] = first + k - taken[0]
            count_ref[s] = at + 1


def tile_copy(tiles_ref, held_ref, came, a, k, i, e):
    return pltpu.make_async_copy(tiles_ref.at[a, k], held_ref.at[i, e], came.at[i, e])


def add_up(s, i, held_ref, count_ref, entry_ref, into_ref, first_ref=None):
    n_entry, width = held_ref.shape[1], held_ref.shape[2]
    named = count_ref[s]

    def tile(m, rows):
        return held_ref[i, entry_ref[s * n_entry + m], rows, :]

    for exact in range(MOST + 1):
        @pl.when(named == exact)
        def _():
            @pl.loop(0, width // STEP)
            def _(r):
                rows = pl.ds(pl.multiple_of(r * STEP, STEP), STEP)
                parts = [] if first_ref is None else [first_ref[rows, :]]
                parts += [tile(m, rows) for m in range(exact)]
                if not parts:
                    total = jnp.zeros((STEP, width), into_ref.dtype)
                elif len(parts) == 2:
                    total = parts[0] + parts[1]
                else:
                    total = parts[0]
                    for part in parts[1:]:
                        total = total.astype(jnp.float32) + part.astype(jnp.float32)
                into_ref[rows, :] = total.astype(into_ref.dtype)

    @pl.when(named > MOST)
    def _():
        @pl.loop(0, width // STEP)
        def _(r):
            rows = pl.ds(pl.multiple_of(r * STEP, STEP), STEP)

            def add(m, total):
                return total + tile(m, rows).astype(jnp.float32)

            total = tile(0, rows) if first_ref is None else first_ref[rows, :]
            first = 1 if first_ref is None else 0
            total = lax.fori_loop(first, named, add, total.astype(jnp.float32))
            into_ref[rows, :] = total.astype(into_ref.dtype)


def add_product(s, i, held_ref, count_ref, entry_ref, sums_ref, amps_ref, total_ref):
    n_entry = held_ref.shape[1]
    named = count_ref[s]

    def multiply(block):
        total_ref[...] += jnp.dot(amps_ref[...], block, preferred_element_type=jnp.float32)

    for exact in range(1, MOST + 1):
        @pl.when(named == exact)
        def _():
            tiles = [held_ref[i, entry_ref[s * n_entry + m]] for m in range(exact)]
            block = tiles[0]
            if exact == 2:
                block = tiles[0] + tiles[1]
            elif exact > 2:
                block = sum(tile.astype(jnp.float32) for tile in tiles).astype(jnp.bfloat16)
            multiply(block)

    @pl.when(named > MOST)
    def _():
        add_up(s, i, held_ref, count_ref, entry_ref, sums_ref)
        multiply(sums_ref[...])


def sums_kernel(vir_ref, chosen_ref, other_ref, tiles_ref, *refs, a, taken, extra):
    sums_ref, there_ref, list_count, list_entry, held_ref, came, count_ref, entry_ref = refs[-8:]
    n_place, per = sums_ref.shape[:2]
    n_own, n_entry = chosen_ref.shape
    n_held = held_ref.shape[1]
    list_entries(vir_ref[0], [(chosen_ref, a, 0, taken, 0)], count_ref, entry_ref, per, n_held)

    @pl.loop(0, n_place * per)
    def _(s):
        @pl.loop(0, count_ref[s])
        def _(m):
            e = entry_ref[s * n_held + m]
            tile_copy(tiles_ref, held_ref, came, a, e + taken[0], 0, e).start()

    there_ref[...] = jnp.zeros_like(there_ref)
    if extra is not None:
        sources = [(other_ref, b, b, range(n_entry), 0) for b in range(n_own)]
        sources += [(chosen_ref, 0, 0, extra, n_entry)] * (len(extra) > 0)
        list_entries(vir_ref[0], sources, list_count, list_entry, per, n_entry + len(extra))

    @pl.loop(0, n_place * per)
    def _(s):
        @pl.loop(0, count_ref[s])
        def _(m):
            e = entry_ref[s * n_held + m]
            tile_copy(tiles_ref, held_ref, came, a, 0, 0, e).wait()

        add_up(s, 0, held_ref, count_ref, entry_ref, sums_ref.at[lax.div(s, per), lax.rem(s, per)])


def tile_sums(vir, chosen, other, tiles, a, taken, extra, per, first):
    n_own, n_entry, width, _ = tiles.shape
    n_place = len(ARRIVAL[0])
    n_tile = n_place * per
    n_list, n_held = (1, 8) if extra is None else (n_own * n_tile, n_entry + len(extra))
    smem, vmem = pl.BlockSpec(memory_space=pltpu.SMEM), pl.BlockSpec(memory_space=pltpu.VMEM)
    return pl.pallas_call(
        functools.partial(sums_kernel, a=a, taken=taken, extra=extra),
        in_specs=[smem] * 3 + [pl.BlockSpec(memory_space=pl.ANY)] * (1 + len(first)),
        out_specs=[vmem] * 2 + [smem] * 2,
        out_shape=[
            jax.ShapeDtypeStruct((n_place, per, width, width), jnp.bfloat16),
            jax.ShapeDtypeStruct((16, 128), jnp.bfloat16),
            jax.ShapeDtypeStruct((n_list,), jnp.int32),
            jax.ShapeDtypeStruct((n_list * n_held,), jnp.int32),
        ],
        scratch_shapes=[
            pltpu.VMEM((1, len(taken), width, width), jnp.bfloat16),
            pltpu.SemaphoreType.DMA((1, len(taken))),
            pltpu.SMEM((n_tile,), jnp.int32),
            pltpu.SMEM((n_tile * len(taken),), jnp.int32),
        ],
        compiler_params=pltpu.CompilerParams(vmem_limit_bytes=44 * MIB),
        cost_estimate=pl.CostEstimate(flops=0, bytes_accessed=1000000, transcendentals=0),
    )(vir, chosen, other, tiles, *first)


def early_kernel(vir_ref, rep_ref, count_ref, entry_ref, occ_ref, pair_ref, mine0_ref, mine1_ref, *refs, extra):
    other_ref, own_ref, refs = refs[0], refs[1], refs[2:]
    pieces, refs = refs[:4 * PIECES], refs[4 * PIECES:]
    total_ref, last_ref, inner_ref, held_ref, came, sums_ref, amps_ref = refs
    mine_refs = (mine0_ref, mine1_ref)
    vir_index = vir_ref[0]
    inner = (vir_index == 1) | (vir_index == 2)
    inner_ref[...] = jnp.full(inner_ref.shape, jnp.where(inner, 1.0, 0.0), jnp.float32)
    n_own, n_held, width, _ = held_ref.shape
    n_entry = n_held - len(extra)
    n_place, per = mine0_ref.shape[:2]

    def slot_of(place, a, t):
        return (a * n_place + place) * per + t

    def start_copies(place):
        for a in range(n_own):
            @pl.loop(0, per)
            def _(t):
                s = slot_of(place, a, t)

                @pl.loop(0, count_ref[s])
                def _(m):
                    e = entry_ref[s * n_held + m]

                    @pl.when(e < n_entry)
                    def _():
                        tile_copy(other_ref, held_ref, came, a, e, a, e).start()

                    if len(extra) and a == 0:
                        @pl.when(e >= n_entry)
                        def _():
                            tile_copy(own_ref, held_ref, came, a, e - n_entry + extra[0], a, e).start()

    def wait_copies(s, a):
        @pl.loop(0, count_ref[s])
        def _(m):
            e = entry_ref[s * n_held + m]
            tile_copy(other_ref, held_ref, came, a, 0, a, e).wait()

    start_copies(n_place - 1)
    pl.loop(0, n_place - 1)(start_copies)

    all_rows, wide = amps_ref.shape[0], per * width
    rows = all_rows // PIECES
    for i in range(PIECES):
        own, near, mid, mid_out = pieces[i::PIECES]
        part = slice(i * rows, (i + 1) * rows)
        amps_ref[part, :wide] = own[...]
        amps_ref[part, wide:2 * wide] = near[...]
        amps_ref[part, 2 * wide:] = jnp.where(inner, mid[...], mid_out[...])
    own_occ = occ_ref[:, :all_rows]
    for rep in range(1, occ_ref.shape[1] // all_rows):
        own_occ = jnp.where(rep_ref[0] == rep, occ_ref[:, rep * all_rows:(rep + 1) * all_rows], own_occ)
    down = jnp.broadcast_to(own_occ, (128, all_rows)).T
    down = jnp.concatenate([down] * (width // 128), axis=1)
    for a in range(n_own):
        columns = slice(a * width, (a + 1) * width)
        gap = pair_ref[:, columns] - down
        total_ref[a] = gap * amps_ref[:, columns].astype(jnp.float32) + jnp.dot(
            amps_ref[...], mine_refs[a][:n_place - 1].reshape(-1, width), preferred_element_type=jnp.float32
        )

    for a in range(n_own):
        @pl.loop(0, per)
        def _(t):
            s = slot_of(n_place - 1, a, t)
            wait_copies(s, a)
            add_up(s, a, held_ref, count_ref, entry_ref, last_ref.at[a, t], mine_refs[a].at[n_place - 1, t])

    @pl.loop(0, n_place - 1)
    def _(place):
        for a in range(n_own):
            @pl.loop(0, per)
            def _(t):
                s = slot_of(place, a, t)
                columns = pl.ds(pl.multiple_of((place * per + t) * width, width), width)
                wait_copies(s, a)
                add_product(
                    s, a, held_ref, count_ref, entry_ref, sums_ref, amps_ref.at[:, columns], total_ref.at[a]
                )


def early_products(vir, rep, count, entry, occ, pair, mine, other, tiles, extra, own, near, mid, mid_out):
    rows, columns = own[0].shape[0] * PIECES, own[0].shape[1]
    n_own, n_entry, width, _ = tiles.shape
    n_place, per = len(ARRIVAL[0]), columns // width
    smem, vmem = pl.BlockSpec(memory_space=pltpu.SMEM), pl.BlockSpec(memory_space=pltpu.VMEM)
    return pl.pallas_call(
        functools.partial(early_kernel, extra=extra),
        in_specs=[smem] * 4 + [vmem] * 4 + [pl.BlockSpec(memory_space=pl.ANY)] * 2 + [vmem] * (4 * PIECES),
        out_specs=[vmem] * 3,
        out_shape=[
            jax.ShapeDtypeStruct((n_own, rows, width), jnp.float32),
            jax.ShapeDtypeStruct((n_own, per, width, width), jnp.bfloat16),
            jax.ShapeDtypeStruct((8, 128), jnp.float32),
        ],
        scratch_shapes=[
            pltpu.VMEM((n_own, n_entry + len(extra), width, width), jnp.bfloat16),
            pltpu.SemaphoreType.DMA((n_own, n_entry + len(extra))),
            pltpu.VMEM((width, width), jnp.bfloat16),
            pltpu.VMEM((rows, (n_place - 1) * columns), jnp.bfloat16),
        ],
        compiler_params=pltpu.CompilerParams(vmem_limit_bytes=34 * MIB),
        cost_estimate=pl.CostEstimate(
            flops=2 * n_place * rows * columns * columns, bytes_accessed=2 * tiles.size, transcendentals=0
        ),
    )(vir, rep, count, entry, occ, pair, *mine, other, tiles, *own, *near, *mid, *mid_out)


def there_kernel(*refs):
    refs[-1][...] = jnp.zeros_like(refs[-1])


def all_there(*arrays):
    return pl.pallas_call(
        there_kernel,
        in_specs=[pl.BlockSpec(memory_space=pl.ANY)] * len(arrays),
        out_specs=pl.BlockSpec(memory_space=pltpu.VMEM),
        out_shape=jax.ShapeDtypeStruct((16, 128), jnp.bfloat16),
        compiler_params=pltpu.CompilerParams(vmem_limit_bytes=MIB),
        cost_estimate=pl.CostEstimate(flops=0, bytes_accessed=1000000, transcendentals=0),
    )(*arrays)


def last_kernel(total_ref, sums_ref, inner_ref, *refs, piece):
    far, far_out_ref, (resid_ref, rows_ref, gone) = refs[:PIECES], refs[PIECES], refs[-3:]
    n_own, _, width, _ = sums_ref.shape
    rows = far_out_ref.shape[0]

    def finish(piece, amps_ref):
        part, held = pl.ds(piece * rows, rows), rows_ref.at[piece]
        for a in range(n_own):
            columns = pl.ds(a * width, width)
            product = jnp.dot(amps_ref[...], sums_ref[a].reshape(-1, width), preferred_element_type=jnp.float32)
            held[:, columns] = (total_ref[a, part] + product).astype(rows_ref.dtype)
            pltpu.make_async_copy(held.at[:, columns], resid_ref.at[part, columns], gone.at[piece, a]).start()

    def wait(piece):
        part, held = pl.ds(piece * rows, rows), rows_ref.at[piece]
        for a in range(n_own):
            columns = pl.ds(a * width, width)
            pltpu.make_async_copy(held.at[:, columns], resid_ref.at[part, columns], gone.at[piece, a]).wait()

    inner = inner_ref[0, 0] > 0

    @pl.when(jnp.logical_not(inner))
    def _():
        finish(piece, far_out_ref)
        wait(piece)

    if piece == 0:
        @pl.when(inner)
        def _():
            for i in range(PIECES):
                finish(i, far[i])
            for i in range(PIECES):
                wait(i)


def last_product(total, sums, inner, far, far_out, piece, resid=None, there=()):
    n_own, rows, width = total.shape
    vmem, anywhere = pl.BlockSpec(memory_space=pltpu.VMEM), pl.BlockSpec(memory_space=pl.ANY)
    others = [*there] if resid is None else [resid, *there]
    shape = (rows, n_own * width)
    return pl.pallas_call(
        functools.partial(last_kernel, piece=piece),
        in_specs=[vmem] * (4 + PIECES) + [anywhere] * len(others),
        out_specs=anywhere,
        out_shape=jax.ShapeDtypeStruct(shape, jnp.bfloat16),
        input_output_aliases={} if resid is None else {4 + PIECES: 0},
        scratch_shapes=[
            pltpu.VMEM((PIECES, rows // PIECES, shape[1]), jnp.bfloat16),
            pltpu.SemaphoreType.DMA((PIECES, n_own)),
        ],
        compiler_params=pltpu.CompilerParams(vmem_limit_bytes=16 * MIB),
        cost_estimate=pl.CostEstimate(flops=0, bytes_accessed=1000000, transcendentals=0),
    )(total, sums, inner, *far, far_out, *others)


def dense_local(amplitudes, integrals, cd_tiles, occ_energy, pair_energy):
    rows = amplitudes.shape[0] // lax.axis_size("rep")
    rep_index, vir_index = lax.axis_index("rep"), lax.axis_index("vir")
    swap_near, swap_mid, outward = [(0, 1), (1, 0), (2, 3), (3, 2)], [(1, 2), (2, 1)], [(1, 0), (2, 3)]
    swap_rep = [(0, 1), (1, 0)]

    def send(pieces, pairs):
        return [lax.ppermute(piece, "vir", pairs) for piece in pieces]

    piece = rows // PIECES
    own = [
        lax.dynamic_slice_in_dim(amplitudes, rep_index * rows + i * piece, piece, 0) for i in range(PIECES)
    ]
    vir, rep = vir_index.reshape(1), rep_index.reshape(1)
    occ, pair = occ_energy[None, :], pair_energy[None, :]
    per = amplitudes.shape[1] // integrals.shape[2]
    marks = []

    def after(mark, *held):
        *held, mark = lax.optimization_barrier((*held, mark))
        marks.append(mark)
        return held

    other = lax.ppermute(integrals, "rep", swap_rep)
    chosen_other = lax.ppermute(cd_tiles, "rep", swap_rep)
    near, mid = send(own, swap_near), send(own, swap_mid)
    n_entry = integrals.shape[1]
    taken, extra = range(n_entry * 8 // 12), range(n_entry * 8 // 12, n_entry)
    mine0, mark, _, _ = tile_sums(vir, cd_tiles, cd_tiles, integrals, 0, taken, None, per, (near[0], mid[0]))
    near[1], mid[1] = after(mark, near[1], mid[1])
    far, mid_out = send(near, swap_mid), send(mid, outward)
    far[0], mid_out[0] = after(all_there(near[1], mid[1]), far[0], mid_out[0])
    mine1, mark, count, entry = tile_sums(
        vir, cd_tiles, chosen_other, integrals, 1, range(n_entry), extra, per, (far[0], mid_out[0])
    )
    mid_out[1], = after(mark, mid_out[1])
    far[1], = after(all_there(mid_out[1]), far[1])
    far_out = send(far, outward)
    total, sums, inner = early_products(
        vir, rep, count, entry, occ, pair, (mine0, mine1), other, integrals, extra, own, near, mid, mid_out
    )
    resid = last_product(total, sums, inner, far, far_out[0], 0, there=marks)
    return last_product(total, sums, inner, far, far_out[1], 1, resid)


def solution(mesh):
    in_specs = (P("occ", "vir"), P("vir", "rep", None, None), P("vir", "rep"), P("occ"), P("vir"))
    out_specs = P(("occ", "rep"), "vir")
    n_rep = mesh.shape["rep"]

    def local(amplitudes, integrals, cd_tiles, occ_energy, pair_energy):
        n_tile = amplitudes.shape[1] * mesh.shape["vir"] // integrals.shape[2]
        few_tiles = n_tile <= n_rep * integrals.shape[1]
        few_tiles &= n_rep == 2 and mesh.shape["vir"] == 4 and integrals.shape[0] == 2 and integrals.shape[1] % 3 == 0
        body = dense_local if few_tiles else sparse_local
        return body(amplitudes, integrals, cd_tiles, occ_energy, pair_energy)

    return jax.shard_map(local, mesh=mesh, in_specs=in_specs, out_specs=out_specs, check_vma=False)
```

```python
import functools

import jax
import jax.numpy as jnp
from jax import lax
from jax.experimental import pallas as pl
from jax.experimental.pallas import tpu as pltpu
from jax.sharding import PartitionSpec as P

MIB = 1024 * 1024


def ladder_tiles(amp_rows, blocks, chosen, tile_width):
    row_count = amp_rows.shape[0]
    tile_view = amp_rows.reshape(row_count, -1, tile_width)
    picked = jnp.take(tile_view, chosen.reshape(-1), axis=1)
    picked = picked.reshape(row_count, chosen.shape[0], chosen.shape[1], tile_width)
    result = jnp.einsum("rakp,akpq->raq", picked, blocks, preferred_element_type=jnp.float32)
    return result.reshape(row_count, -1)


def sparse_local(amplitudes, integrals, cd_tiles, occ_energy, pair_energy):
    tile_width = integrals.shape[2]
    own_rows = amplitudes.shape[0]
    rep_rows = own_rows // lax.axis_size("rep")
    rep_index = lax.axis_index("rep")
    own_amps = lax.dynamic_slice_in_dim(amplitudes, rep_index * rep_rows, rep_rows, 0)
    whole = lax.all_gather(amplitudes, "vir", axis=1, tiled=True)
    partial_value = ladder_tiles(whole, integrals, cd_tiles, tile_width)
    sums = lax.psum_scatter(
        partial_value.astype(jnp.bfloat16), "rep", scatter_dimension=0, tiled=True
    ).astype(jnp.float32)
    own_occ = lax.dynamic_slice_in_dim(occ_energy, rep_index * rep_rows, rep_rows, 0)
    energy_gap = pair_energy[None, :] - own_occ[:, None]
    return (sums + energy_gap * own_amps.astype(jnp.float32)).astype(jnp.bfloat16)


ARRIVAL = ((0, 1, 2, 3), (1, 0, 2, 3), (2, 3, 1, 0), (3, 2, 1, 0))
PIECES = 2
STEP = 128
MOST = 4


def arrival_of(vir_index, place):
    chunk = jnp.int32(0)
    for index, chunks in enumerate(ARRIVAL):
        chunk = jnp.where(vir_index == index, chunks[place], chunk)
    return chunk


def list_entries(vir_index, sources, count_ref, entry_ref, per, n_held):
    n_place = len(ARRIVAL[0])
    places = [jnp.int32(0)] * n_place
    for place in range(n_place):
        for chunk in range(n_place):
            places[chunk] = jnp.where(arrival_of(vir_index, place) == chunk, place, places[chunk])

    @pl.loop(0, count_ref.shape[0])
    def _(s):
        count_ref[s] = 0

    for chosen_ref, a, i, taken, first in sources:
        for k in taken:
            tile = chosen_ref[a, k]
            chunk = lax.div(tile, per)
            place = places[0]
            for other in range(1, n_place):
                place = jnp.where(chunk == other, places[other], place)
            s = (i * n_place + place) * per + lax.rem(tile, per)
            at = count_ref[s]
            entry_ref[s * n_held + at] = first + k - taken[0]
            count_ref[s] = at + 1


def tile_copy(tiles_ref, held_ref, came, a, k, i, e):
    return pltpu.make_async_copy(tiles_ref.at[a, k], held_ref.at[i, e], came.at[i, e])


def add_up(s, i, held_ref, count_ref, entry_ref, into_ref, first_ref=None):
    n_entry, width = held_ref.shape[1], held_ref.shape[2]
    named = count_ref[s]

    def tile(m, rows):
        return held_ref[i, entry_ref[s * n_entry + m], rows, :]

    for exact in range(MOST + 1):
        @pl.when(named == exact)
        def _():
            @pl.loop(0, width // STEP)
            def _(r):
                rows = pl.ds(pl.multiple_of(r * STEP, STEP), STEP)
                parts = [] if first_ref is None else [first_ref[rows, :]]
                parts += [tile(m, rows) for m in range(exact)]
                if not parts:
                    total = jnp.zeros((STEP, width), into_ref.dtype)
                elif len(parts) == 2:
                    total = parts[0] + parts[1]
                else:
                    total = parts[0]
                    for part in parts[1:]:
                        total = total.astype(jnp.float32) + part.astype(jnp.float32)
                into_ref[rows, :] = total.astype(into_ref.dtype)

    @pl.when(named > MOST)
    def _():
        @pl.loop(0, width // STEP)
        def _(r):
            rows = pl.ds(pl.multiple_of(r * STEP, STEP), STEP)

            def add(m, total):
                return total + tile(m, rows).astype(jnp.float32)

            total = tile(0, rows) if first_ref is None else first_ref[rows, :]
            first = 1 if first_ref is None else 0
            total = lax.fori_loop(first, named, add, total.astype(jnp.float32))
            into_ref[rows, :] = total.astype(into_ref.dtype)


def add_product(s, i, held_ref, count_ref, entry_ref, sums_ref, amps_ref, total_ref):
    n_entry = held_ref.shape[1]
    named = count_ref[s]

    def multiply(block):
        total_ref[...] += jnp.dot(amps_ref[...], block, preferred_element_type=jnp.float32)

    for exact in range(1, MOST + 1):
        @pl.when(named == exact)
        def _():
            tiles = [held_ref[i, entry_ref[s * n_entry + m]] for m in range(exact)]
            block = tiles[0]
            if exact == 2:
                block = tiles[0] + tiles[1]
            elif exact > 2:
                block = sum(tile.astype(jnp.float32) for tile in tiles).astype(jnp.bfloat16)
            multiply(block)

    @pl.when(named > MOST)
    def _():
        add_up(s, i, held_ref, count_ref, entry_ref, sums_ref)
        multiply(sums_ref[...])


def sums_kernel(vir_ref, chosen_ref, other_ref, tiles_ref, *refs, a, taken, extra):
    sums_ref, there_ref, list_count, list_entry, held_ref, came, count_ref, entry_ref = refs[-8:]
    n_place, per = sums_ref.shape[:2]
    n_own, n_entry = chosen_ref.shape
    n_held = held_ref.shape[1]
    list_entries(vir_ref[0], [(chosen_ref, a, 0, taken, 0)], count_ref, entry_ref, per, n_held)

    @pl.loop(0, n_place * per)
    def _(s):
        @pl.loop(0, count_ref[s])
        def _(m):
            e = entry_ref[s * n_held + m]
            tile_copy(tiles_ref, held_ref, came, a, e + taken[0], 0, e).start()

    there_ref[...] = jnp.zeros_like(there_ref)
    if extra is not None:
        sources = [(other_ref, b, b, range(n_entry), 0) for b in range(n_own)]
        sources += [(chosen_ref, 0, 0, extra, n_entry)] * (len(extra) > 0)
        list_entries(vir_ref[0], sources, list_count, list_entry, per, n_entry + len(extra))

    @pl.loop(0, n_place * per)
    def _(s):
        @pl.loop(0, count_ref[s])
        def _(m):
            e = entry_ref[s * n_held + m]
            tile_copy(tiles_ref, held_ref, came, a, 0, 0, e).wait()

        add_up(s, 0, held_ref, count_ref, entry_ref, sums_ref.at[lax.div(s, per), lax.rem(s, per)])


def tile_sums(vir, chosen, other, tiles, a, taken, extra, per, first):
    n_own, n_entry, width, _ = tiles.shape
    n_place = len(ARRIVAL[0])
    n_tile = n_place * per
    n_list, n_held = (1, 8) if extra is None else (n_own * n_tile, n_entry + len(extra))
    smem, vmem = pl.BlockSpec(memory_space=pltpu.SMEM), pl.BlockSpec(memory_space=pltpu.VMEM)
    return pl.pallas_call(
        functools.partial(sums_kernel, a=a, taken=taken, extra=extra),
        in_specs=[smem] * 3 + [pl.BlockSpec(memory_space=pl.ANY)] * (1 + len(first)),
        out_specs=[vmem] * 2 + [smem] * 2,
        out_shape=[
            jax.ShapeDtypeStruct((n_place, per, width, width), jnp.bfloat16),
            jax.ShapeDtypeStruct((16, 128), jnp.bfloat16),
            jax.ShapeDtypeStruct((n_list,), jnp.int32),
            jax.ShapeDtypeStruct((n_list * n_held,), jnp.int32),
        ],
        scratch_shapes=[
            pltpu.VMEM((1, len(taken), width, width), jnp.bfloat16),
            pltpu.SemaphoreType.DMA((1, len(taken))),
            pltpu.SMEM((n_tile,), jnp.int32),
            pltpu.SMEM((n_tile * len(taken),), jnp.int32),
        ],
        compiler_params=pltpu.CompilerParams(vmem_limit_bytes=44 * MIB),
        cost_estimate=pl.CostEstimate(flops=0, bytes_accessed=1000000, transcendentals=0),
    )(vir, chosen, other, tiles, *first)


def early_kernel(vir_ref, rep_ref, count_ref, entry_ref, occ_ref, pair_ref, mine0_ref, mine1_ref, *refs, extra):
    other_ref, own_ref, refs = refs[0], refs[1], refs[2:]
    pieces, refs = refs[:4 * PIECES], refs[4 * PIECES:]
    total_ref, last_ref, inner_ref, held_ref, came, sums_ref, amps_ref = refs
    mine_refs = (mine0_ref, mine1_ref)
    vir_index = vir_ref[0]
    inner = (vir_index == 1) | (vir_index == 2)
    inner_ref[...] = jnp.full(inner_ref.shape, jnp.where(inner, 1.0, 0.0), jnp.float32)
    n_own, n_held, width, _ = held_ref.shape
    n_entry = n_held - len(extra)
    n_place, per = mine0_ref.shape[:2]

    def slot_of(place, a, t):
        return (a * n_place + place) * per + t

    def start_copies(place):
        for a in range(n_own):
            @pl.loop(0, per)
            def _(t):
                s = slot_of(place, a, t)

                @pl.loop(0, count_ref[s])
                def _(m):
                    e = entry_ref[s * n_held + m]

                    @pl.when(e < n_entry)
                    def _():
                        tile_copy(other_ref, held_ref, came, a, e, a, e).start()

                    if len(extra) and a == 0:
                        @pl.when(e >= n_entry)
                        def _():
                            tile_copy(own_ref, held_ref, came, a, e - n_entry + extra[0], a, e).start()

    def wait_copies(s, a):
        @pl.loop(0, count_ref[s])
        def _(m):
            e = entry_ref[s * n_held + m]
            tile_copy(other_ref, held_ref, came, a, 0, a, e).wait()

    start_copies(n_place - 1)
    pl.loop(0, n_place - 1)(start_copies)

    all_rows, wide = amps_ref.shape[0], per * width
    rows = all_rows // PIECES
    for i in range(PIECES):
        own, near, mid, mid_out = pieces[i::PIECES]
        part = slice(i * rows, (i + 1) * rows)
        amps_ref[part, :wide] = own[...]
        amps_ref[part, wide:2 * wide] = near[...]
        amps_ref[part, 2 * wide:] = jnp.where(inner, mid[...], mid_out[...])
    own_occ = occ_ref[:, :all_rows]
    for rep in range(1, occ_ref.shape[1] // all_rows):
        own_occ = jnp.where(rep_ref[0] == rep, occ_ref[:, rep * all_rows:(rep + 1) * all_rows], own_occ)
    down = jnp.broadcast_to(own_occ, (128, all_rows)).T
    down = jnp.concatenate([down] * (width // 128), axis=1)
    for a in range(n_own):
        columns = slice(a * width, (a + 1) * width)
        gap = pair_ref[:, columns] - down
        total_ref[a] = gap * amps_ref[:, columns].astype(jnp.float32) + jnp.dot(
            amps_ref[...], mine_refs[a][:n_place - 1].reshape(-1, width), preferred_element_type=jnp.float32
        )

    for a in range(n_own):
        @pl.loop(0, per)
        def _(t):
            s = slot_of(n_place - 1, a, t)
            wait_copies(s, a)
            add_up(s, a, held_ref, count_ref, entry_ref, last_ref.at[a, t], mine_refs[a].at[n_place - 1, t])

    @pl.loop(0, n_place - 1)
    def _(place):
        for a in range(n_own):
            @pl.loop(0, per)
            def _(t):
                s = slot_of(place, a, t)
                columns = pl.ds(pl.multiple_of((place * per + t) * width, width), width)
                wait_copies(s, a)
                add_product(
                    s, a, held_ref, count_ref, entry_ref, sums_ref, amps_ref.at[:, columns], total_ref.at[a]
                )


def early_products(vir, rep, count, entry, occ, pair, mine, other, tiles, extra, own, near, mid, mid_out):
    rows, columns = own[0].shape[0] * PIECES, own[0].shape[1]
    n_own, n_entry, width, _ = tiles.shape
    n_place, per = len(ARRIVAL[0]), columns // width
    smem, vmem = pl.BlockSpec(memory_space=pltpu.SMEM), pl.BlockSpec(memory_space=pltpu.VMEM)
    return pl.pallas_call(
        functools.partial(early_kernel, extra=extra),
        in_specs=[smem] * 4 + [vmem] * 4 + [pl.BlockSpec(memory_space=pl.ANY)] * 2 + [vmem] * (4 * PIECES),
        out_specs=[vmem] * 3,
        out_shape=[
            jax.ShapeDtypeStruct((n_own, rows, width), jnp.float32),
            jax.ShapeDtypeStruct((n_own, per, width, width), jnp.bfloat16),
            jax.ShapeDtypeStruct((8, 128), jnp.float32),
        ],
        scratch_shapes=[
            pltpu.VMEM((n_own, n_entry + len(extra), width, width), jnp.bfloat16),
            pltpu.SemaphoreType.DMA((n_own, n_entry + len(extra))),
            pltpu.VMEM((width, width), jnp.bfloat16),
            pltpu.VMEM((rows, (n_place - 1) * columns), jnp.bfloat16),
        ],
        compiler_params=pltpu.CompilerParams(vmem_limit_bytes=34 * MIB),
        cost_estimate=pl.CostEstimate(
            flops=2 * n_place * rows * columns * columns, bytes_accessed=2 * tiles.size, transcendentals=0
        ),
    )(vir, rep, count, entry, occ, pair, *mine, other, tiles, *own, *near, *mid, *mid_out)


def there_kernel(*refs):
    refs[-1][...] = jnp.zeros_like(refs[-1])


def all_there(*arrays):
    return pl.pallas_call(
        there_kernel,
        in_specs=[pl.BlockSpec(memory_space=pl.ANY)] * len(arrays),
        out_specs=pl.BlockSpec(memory_space=pltpu.VMEM),
        out_shape=jax.ShapeDtypeStruct((16, 128), jnp.bfloat16),
        compiler_params=pltpu.CompilerParams(vmem_limit_bytes=MIB),
        cost_estimate=pl.CostEstimate(flops=0, bytes_accessed=1000000, transcendentals=0),
    )(*arrays)


def last_kernel(total_ref, sums_ref, inner_ref, *refs, piece):
    far, far_out_ref, (resid_ref, rows_ref, gone) = refs[:PIECES], refs[PIECES], refs[-3:]
    n_own, _, width, _ = sums_ref.shape
    rows = far_out_ref.shape[0]

    def finish(piece, amps_ref):
        part, held = pl.ds(piece * rows, rows), rows_ref.at[piece]
        for a in range(n_own):
            columns = pl.ds(a * width, width)
            product = jnp.dot(amps_ref[...], sums_ref[a].reshape(-1, width), preferred_element_type=jnp.float32)
            held[:, columns] = (total_ref[a, part] + product).astype(rows_ref.dtype)
            pltpu.make_async_copy(held.at[:, columns], resid_ref.at[part, columns], gone.at[piece, a]).start()

    def wait(piece):
        part, held = pl.ds(piece * rows, rows), rows_ref.at[piece]
        for a in range(n_own):
            columns = pl.ds(a * width, width)
            pltpu.make_async_copy(held.at[:, columns], resid_ref.at[part, columns], gone.at[piece, a]).wait()

    inner = inner_ref[0, 0] > 0

    @pl.when(jnp.logical_not(inner))
    def _():
        finish(piece, far_out_ref)
        wait(piece)

    if piece == 0:
        @pl.when(inner)
        def _():
            for i in range(PIECES):
                finish(i, far[i])
            for i in range(PIECES):
                wait(i)


def last_product(total, sums, inner, far, far_out, piece, resid=None, there=()):
    n_own, rows, width = total.shape
    vmem, anywhere = pl.BlockSpec(memory_space=pltpu.VMEM), pl.BlockSpec(memory_space=pl.ANY)
    others = [*there] if resid is None else [resid, *there]
    shape = (rows, n_own * width)
    return pl.pallas_call(
        functools.partial(last_kernel, piece=piece),
        in_specs=[vmem] * (4 + PIECES) + [anywhere] * len(others),
        out_specs=anywhere,
        out_shape=jax.ShapeDtypeStruct(shape, jnp.bfloat16),
        input_output_aliases={} if resid is None else {4 + PIECES: 0},
        scratch_shapes=[
            pltpu.VMEM((PIECES, rows // PIECES, shape[1]), jnp.bfloat16),
            pltpu.SemaphoreType.DMA((PIECES, n_own)),
        ],
        compiler_params=pltpu.CompilerParams(vmem_limit_bytes=16 * MIB),
        cost_estimate=pl.CostEstimate(flops=0, bytes_accessed=1000000, transcendentals=0),
    )(total, sums, inner, *far, far_out, *others)


def dense_local(amplitudes, integrals, cd_tiles, occ_energy, pair_energy):
    rows = amplitudes.shape[0] // lax.axis_size("rep")
    rep_index, vir_index = lax.axis_index("rep"), lax.axis_index("vir")
    swap_near, swap_mid, outward = [(0, 1), (1, 0), (2, 3), (3, 2)], [(1, 2), (2, 1)], [(1, 0), (2, 3)]
    swap_rep = [(0, 1), (1, 0)]

    def send(pieces, pairs):
        return [lax.ppermute(piece, "vir", pairs) for piece in pieces]

    piece = rows // PIECES
    own = [
        lax.dynamic_slice_in_dim(amplitudes, rep_index * rows + i * piece, piece, 0) for i in range(PIECES)
    ]
    vir, rep = vir_index.reshape(1), rep_index.reshape(1)
    occ, pair = occ_energy[None, :], pair_energy[None, :]
    per = amplitudes.shape[1] // integrals.shape[2]
    marks = []

    def after(mark, *held):
        *held, mark = lax.optimization_barrier((*held, mark))
        marks.append(mark)
        return held

    chosen_other = lax.ppermute(cd_tiles, "rep", swap_rep)
    *own, tiles, chosen_other = lax.optimization_barrier((*own, integrals, chosen_other))
    other = lax.ppermute(tiles, "rep", swap_rep)
    near, mid = send(own, swap_near), send(own, swap_mid)
    n_entry = integrals.shape[1]
    taken, extra = range(n_entry), range(n_entry, n_entry)
    mine0, mark, _, _ = tile_sums(vir, cd_tiles, cd_tiles, integrals, 0, taken, None, per, (near[0], mid[0]))
    near[1], mid[1] = after(mark, near[1], mid[1])
    far, mid_out = send(near, swap_mid), send(mid, outward)
    far[0], mid_out[0] = after(all_there(near[1], mid[1]), far[0], mid_out[0])
    mine1, mark, count, entry = tile_sums(
        vir, cd_tiles, chosen_other, integrals, 1, range(n_entry), extra, per, (far[0], mid_out[0])
    )
    mid_out[1], = after(mark, mid_out[1])
    far[1], = after(all_there(mid_out[1]), far[1])
    far_out = send(far, outward)
    total, sums, inner = early_products(
        vir, rep, count, entry, occ, pair, (mine0, mine1), other, integrals, extra, own, near, mid, mid_out
    )
    resid = last_product(total, sums, inner, far, far_out[0], 0, there=marks)
    return last_product(total, sums, inner, far, far_out[1], 1, resid)


def solution(mesh):
    in_specs = (P("occ", "vir"), P("vir", "rep", None, None), P("vir", "rep"), P("occ"), P("vir"))
    out_specs = P(("occ", "rep"), "vir")
    n_rep = mesh.shape["rep"]

    def local(amplitudes, integrals, cd_tiles, occ_energy, pair_energy):
        n_tile = amplitudes.shape[1] * mesh.shape["vir"] // integrals.shape[2]
        few_tiles = n_tile <= n_rep * integrals.shape[1]
        few_tiles &= n_rep == 2 and mesh.shape["vir"] == 4 and integrals.shape[0] == 2 and integrals.shape[1] % 3 == 0
        body = dense_local if few_tiles else sparse_local
        return body(amplitudes, integrals, cd_tiles, occ_energy, pair_energy)

    return jax.shard_map(local, mesh=mesh, in_specs=in_specs, out_specs=out_specs, check_vma=False)
```

```python
import functools

import jax
import jax.numpy as jnp
from jax import lax
from jax.experimental import pallas as pl
from jax.experimental.pallas import tpu as pltpu
from jax.sharding import PartitionSpec as P

MIB = 1024 * 1024


def ladder_tiles(amp_rows, blocks, chosen, tile_width):
    row_count = amp_rows.shape[0]
    tile_view = amp_rows.reshape(row_count, -1, tile_width)
    picked = jnp.take(tile_view, chosen.reshape(-1), axis=1)
    picked = picked.reshape(row_count, chosen.shape[0], chosen.shape[1], tile_width)
    result = jnp.einsum("rakp,akpq->raq", picked, blocks, preferred_element_type=jnp.float32)
    return result.reshape(row_count, -1)


def sparse_local(amplitudes, integrals, cd_tiles, occ_energy, pair_energy):
    tile_width = integrals.shape[2]
    own_rows = amplitudes.shape[0]
    rep_rows = own_rows // lax.axis_size("rep")
    rep_index = lax.axis_index("rep")
    own_amps = lax.dynamic_slice_in_dim(amplitudes, rep_index * rep_rows, rep_rows, 0)
    whole = lax.all_gather(amplitudes, "vir", axis=1, tiled=True)
    partial_value = ladder_tiles(whole, integrals, cd_tiles, tile_width)
    sums = lax.psum_scatter(
        partial_value.astype(jnp.bfloat16), "rep", scatter_dimension=0, tiled=True
    ).astype(jnp.float32)
    own_occ = lax.dynamic_slice_in_dim(occ_energy, rep_index * rep_rows, rep_rows, 0)
    energy_gap = pair_energy[None, :] - own_occ[:, None]
    return (sums + energy_gap * own_amps.astype(jnp.float32)).astype(jnp.bfloat16)


ARRIVAL = ((0, 1, 2, 3), (1, 0, 2, 3), (2, 3, 1, 0), (3, 2, 1, 0))
PIECES = 2
STEP = 128
MOST = 4


def arrival_of(vir_index, place):
    chunk = jnp.int32(0)
    for index, chunks in enumerate(ARRIVAL):
        chunk = jnp.where(vir_index == index, chunks[place], chunk)
    return chunk


def list_entries(vir_index, sources, count_ref, entry_ref, per, n_held):
    n_place = len(ARRIVAL[0])
    places = [jnp.int32(0)] * n_place
    for place in range(n_place):
        for chunk in range(n_place):
            places[chunk] = jnp.where(arrival_of(vir_index, place) == chunk, place, places[chunk])

    @pl.loop(0, count_ref.shape[0])
    def _(s):
        count_ref[s] = 0

    for chosen_ref, a, i, taken, first in sources:
        for k in taken:
            tile = chosen_ref[a, k]
            chunk = lax.div(tile, per)
            place = places[0]
            for other in range(1, n_place):
                place = jnp.where(chunk == other, places[other], place)
            s = (i * n_place + place) * per + lax.rem(tile, per)
            at = count_ref[s]
            entry_ref[s * n_held + at] = first + k - taken[0]
            count_ref[s] = at + 1


def tile_copy(tiles_ref, held_ref, came, a, k, i, e):
    return pltpu.make_async_copy(tiles_ref.at[a, k], held_ref.at[i, e], came.at[i, e])


def add_up(s, i, held_ref, count_ref, entry_ref, into_ref, first_ref=None):
    n_entry, width = held_ref.shape[1], held_ref.shape[2]
    named = count_ref[s]

    def tile(m, rows):
        return held_ref[i, entry_ref[s * n_entry + m], rows, :]

    for exact in range(MOST + 1):
        @pl.when(named == exact)
        def _():
            @pl.loop(0, width // STEP)
            def _(r):
                rows = pl.ds(pl.multiple_of(r * STEP, STEP), STEP)
                parts = [] if first_ref is None else [first_ref[rows, :]]
                parts += [tile(m, rows) for m in range(exact)]
                if not parts:
                    total = jnp.zeros((STEP, width), into_ref.dtype)
                elif len(parts) == 2:
                    total = parts[0] + parts[1]
                else:
                    total = parts[0]
                    for part in parts[1:]:
                        total = total.astype(jnp.float32) + part.astype(jnp.float32)
                into_ref[rows, :] = total.astype(into_ref.dtype)

    @pl.when(named > MOST)
    def _():
        @pl.loop(0, width // STEP)
        def _(r):
            rows = pl.ds(pl.multiple_of(r * STEP, STEP), STEP)

            def add(m, total):
                return total + tile(m, rows).astype(jnp.float32)

            total = tile(0, rows) if first_ref is None else first_ref[rows, :]
            first = 1 if first_ref is None else 0
            total = lax.fori_loop(first, named, add, total.astype(jnp.float32))
            into_ref[rows, :] = total.astype(into_ref.dtype)


def add_product(s, i, held_ref, count_ref, entry_ref, sums_ref, amps_ref, total_ref):
    n_entry = held_ref.shape[1]
    named = count_ref[s]

    def multiply(block):
        total_ref[...] += jnp.dot(amps_ref[...], block, preferred_element_type=jnp.float32)

    for exact in range(1, MOST + 1):
        @pl.when(named == exact)
        def _():
            tiles = [held_ref[i, entry_ref[s * n_entry + m]] for m in range(exact)]
            block = tiles[0]
            if exact == 2:
                block = tiles[0] + tiles[1]
            elif exact > 2:
                block = sum(tile.astype(jnp.float32) for tile in tiles).astype(jnp.bfloat16)
            multiply(block)

    @pl.when(named > MOST)
    def _():
        add_up(s, i, held_ref, count_ref, entry_ref, sums_ref)
        multiply(sums_ref[...])


def sums_kernel(vir_ref, chosen_ref, other_ref, tiles_ref, *refs, a, taken, extra):
    sums_ref, there_ref, list_count, list_entry, held_ref, came, count_ref, entry_ref = refs[-8:]
    n_place, per = sums_ref.shape[:2]
    n_own, n_entry = chosen_ref.shape
    n_held = held_ref.shape[1]
    list_entries(vir_ref[0], [(chosen_ref, a, 0, taken, 0)], count_ref, entry_ref, per, n_held)

    @pl.loop(0, n_place * per)
    def _(s):
        @pl.loop(0, count_ref[s])
        def _(m):
            e = entry_ref[s * n_held + m]
            tile_copy(tiles_ref, held_ref, came, a, e + taken[0], 0, e).start()

    there_ref[...] = jnp.zeros_like(there_ref)
    if extra is not None:
        sources = [(other_ref, b, b, range(n_entry), 0) for b in range(n_own)]
        sources += [(chosen_ref, 0, 0, extra, n_entry)] * (len(extra) > 0)
        list_entries(vir_ref[0], sources, list_count, list_entry, per, n_entry + len(extra))

    @pl.loop(0, n_place * per)
    def _(s):
        @pl.loop(0, count_ref[s])
        def _(m):
            e = entry_ref[s * n_held + m]
            tile_copy(tiles_ref, held_ref, came, a, 0, 0, e).wait()

        add_up(s, 0, held_ref, count_ref, entry_ref, sums_ref.at[lax.div(s, per), lax.rem(s, per)])


def tile_sums(vir, chosen, other, tiles, a, taken, extra, per, first):
    n_own, n_entry, width, _ = tiles.shape
    n_place = len(ARRIVAL[0])
    n_tile = n_place * per
    n_list, n_held = (1, 8) if extra is None else (n_own * n_tile, n_entry + len(extra))
    smem, vmem = pl.BlockSpec(memory_space=pltpu.SMEM), pl.BlockSpec(memory_space=pltpu.VMEM)
    return pl.pallas_call(
        functools.partial(sums_kernel, a=a, taken=taken, extra=extra),
        in_specs=[smem] * 3 + [pl.BlockSpec(memory_space=pl.ANY)] * (1 + len(first)),
        out_specs=[vmem] * 2 + [smem] * 2,
        out_shape=[
            jax.ShapeDtypeStruct((n_place, per, width, width), jnp.bfloat16),
            jax.ShapeDtypeStruct((16, 128), jnp.bfloat16),
            jax.ShapeDtypeStruct((n_list,), jnp.int32),
            jax.ShapeDtypeStruct((n_list * n_held,), jnp.int32),
        ],
        scratch_shapes=[
            pltpu.VMEM((1, len(taken), width, width), jnp.bfloat16),
            pltpu.SemaphoreType.DMA((1, len(taken))),
            pltpu.SMEM((n_tile,), jnp.int32),
            pltpu.SMEM((n_tile * len(taken),), jnp.int32),
        ],
        compiler_params=pltpu.CompilerParams(vmem_limit_bytes=44 * MIB),
        cost_estimate=pl.CostEstimate(flops=0, bytes_accessed=1000000, transcendentals=0),
    )(vir, chosen, other, tiles, *first)


def early_kernel(vir_ref, rep_ref, count_ref, entry_ref, occ_ref, pair_ref, mine0_ref, mine1_ref, *refs, extra):
    other_ref, own_ref, refs = refs[0], refs[1], refs[2:]
    pieces, refs = refs[:4 * PIECES], refs[4 * PIECES:]
    total_ref, last_ref, inner_ref, held_ref, came, sums_ref, amps_ref = refs
    mine_refs = (mine0_ref, mine1_ref)
    vir_index = vir_ref[0]
    inner = (vir_index == 1) | (vir_index == 2)
    inner_ref[...] = jnp.full(inner_ref.shape, jnp.where(inner, 1.0, 0.0), jnp.float32)
    n_own, n_held, width, _ = held_ref.shape
    n_entry = n_held - len(extra)
    n_place, per = mine0_ref.shape[:2]

    def slot_of(place, a, t):
        return (a * n_place + place) * per + t

    def start_copies(place):
        for a in range(n_own):
            @pl.loop(0, per)
            def _(t):
                s = slot_of(place, a, t)

                @pl.loop(0, count_ref[s])
                def _(m):
                    e = entry_ref[s * n_held + m]

                    @pl.when(e < n_entry)
                    def _():
                        tile_copy(other_ref, held_ref, came, a, e, a, e).start()

                    if len(extra) and a == 0:
                        @pl.when(e >= n_entry)
                        def _():
                            tile_copy(own_ref, held_ref, came, a, e - n_entry + extra[0], a, e).start()

    def wait_copies(s, a):
        @pl.loop(0, count_ref[s])
        def _(m):
            e = entry_ref[s * n_held + m]
            tile_copy(other_ref, held_ref, came, a, 0, a, e).wait()

    start_copies(n_place - 1)
    pl.loop(0, n_place - 1)(start_copies)

    all_rows, wide = amps_ref.shape[0], per * width
    rows = all_rows // PIECES
    for i in range(PIECES):
        own, near, mid, mid_out = pieces[i::PIECES]
        part = slice(i * rows, (i + 1) * rows)
        amps_ref[part, :wide] = own[...]
        amps_ref[part, wide:2 * wide] = near[...]
        amps_ref[part, 2 * wide:] = jnp.where(inner, mid[...], mid_out[...])
    own_occ = occ_ref[:, :all_rows]
    for rep in range(1, occ_ref.shape[1] // all_rows):
        own_occ = jnp.where(rep_ref[0] == rep, occ_ref[:, rep * all_rows:(rep + 1) * all_rows], own_occ)
    down = jnp.broadcast_to(own_occ, (128, all_rows)).T
    down = jnp.concatenate([down] * (width // 128), axis=1)
    for a in range(n_own):
        columns = slice(a * width, (a + 1) * width)
        gap = pair_ref[:, columns] - down
        total_ref[a] = gap * amps_ref[:, columns].astype(jnp.float32) + jnp.dot(
            amps_ref[...], mine_refs[a][:n_place - 1].reshape(-1, width), preferred_element_type=jnp.float32
        )

    for a in range(n_own):
        @pl.loop(0, per)
        def _(t):
            s = slot_of(n_place - 1, a, t)
            wait_copies(s, a)
            add_up(s, a, held_ref, count_ref, entry_ref, last_ref.at[a, t], mine_refs[a].at[n_place - 1, t])

    @pl.loop(0, n_place - 1)
    def _(place):
        for a in range(n_own):
            @pl.loop(0, per)
            def _(t):
                s = slot_of(place, a, t)
                columns = pl.ds(pl.multiple_of((place * per + t) * width, width), width)
                wait_copies(s, a)
                add_product(
                    s, a, held_ref, count_ref, entry_ref, sums_ref, amps_ref.at[:, columns], total_ref.at[a]
                )


def early_products(vir, rep, count, entry, occ, pair, mine, other, tiles, extra, own, near, mid, mid_out):
    rows, columns = own[0].shape[0] * PIECES, own[0].shape[1]
    n_own, n_entry, width, _ = tiles.shape
    n_place, per = len(ARRIVAL[0]), columns // width
    smem, vmem = pl.BlockSpec(memory_space=pltpu.SMEM), pl.BlockSpec(memory_space=pltpu.VMEM)
    return pl.pallas_call(
        functools.partial(early_kernel, extra=extra),
        in_specs=[smem] * 4 + [vmem] * 4 + [pl.BlockSpec(memory_space=pl.ANY)] * 2 + [vmem] * (4 * PIECES),
        out_specs=[vmem] * 3,
        out_shape=[
            jax.ShapeDtypeStruct((n_own, rows, width), jnp.float32),
            jax.ShapeDtypeStruct((n_own, per, width, width), jnp.bfloat16),
            jax.ShapeDtypeStruct((8, 128), jnp.float32),
        ],
        scratch_shapes=[
            pltpu.VMEM((n_own, n_entry + len(extra), width, width), jnp.bfloat16),
            pltpu.SemaphoreType.DMA((n_own, n_entry + len(extra))),
            pltpu.VMEM((width, width), jnp.bfloat16),
            pltpu.VMEM((rows, (n_place - 1) * columns), jnp.bfloat16),
        ],
        compiler_params=pltpu.CompilerParams(vmem_limit_bytes=34 * MIB),
        cost_estimate=pl.CostEstimate(
            flops=2 * n_place * rows * columns * columns, bytes_accessed=2 * tiles.size, transcendentals=0
        ),
    )(vir, rep, count, entry, occ, pair, *mine, other, tiles, *own, *near, *mid, *mid_out)


def there_kernel(*refs):
    refs[-1][...] = jnp.zeros_like(refs[-1])


def near_by_kernel(array_ref, *refs):
    copy_ref, there_ref = refs[-2:]
    copy_ref[...] = array_ref[...]
    there_ref[...] = jnp.zeros_like(there_ref)


def near_by(array, *first):
    vmem = pl.BlockSpec(memory_space=pltpu.VMEM)
    return pl.pallas_call(
        near_by_kernel,
        in_specs=[vmem] + [pl.BlockSpec(memory_space=pl.ANY)] * len(first),
        out_specs=[vmem] * 2,
        out_shape=[
            jax.ShapeDtypeStruct(array.shape, array.dtype), jax.ShapeDtypeStruct((16, 128), jnp.bfloat16)
        ],
        compiler_params=pltpu.CompilerParams(vmem_limit_bytes=MIB),
        cost_estimate=pl.CostEstimate(flops=0, bytes_accessed=1000000, transcendentals=0),
    )(array, *first)


def all_there(*arrays):
    return pl.pallas_call(
        there_kernel,
        in_specs=[pl.BlockSpec(memory_space=pl.ANY)] * len(arrays),
        out_specs=pl.BlockSpec(memory_space=pltpu.VMEM),
        out_shape=jax.ShapeDtypeStruct((16, 128), jnp.bfloat16),
        compiler_params=pltpu.CompilerParams(vmem_limit_bytes=MIB),
        cost_estimate=pl.CostEstimate(flops=0, bytes_accessed=1000000, transcendentals=0),
    )(*arrays)


def last_kernel(total_ref, sums_ref, inner_ref, *refs, piece):
    far, far_out_ref, (resid_ref, rows_ref, gone) = refs[:PIECES], refs[PIECES], refs[-3:]
    n_own, _, width, _ = sums_ref.shape
    rows = far_out_ref.shape[0]

    def finish(piece, amps_ref):
        part, held = pl.ds(piece * rows, rows), rows_ref.at[piece]
        for a in range(n_own):
            columns = pl.ds(a * width, width)
            product = jnp.dot(amps_ref[...], sums_ref[a].reshape(-1, width), preferred_element_type=jnp.float32)
            held[:, columns] = (total_ref[a, part] + product).astype(rows_ref.dtype)
            pltpu.make_async_copy(held.at[:, columns], resid_ref.at[part, columns], gone.at[piece, a]).start()

    def wait(piece):
        part, held = pl.ds(piece * rows, rows), rows_ref.at[piece]
        for a in range(n_own):
            columns = pl.ds(a * width, width)
            pltpu.make_async_copy(held.at[:, columns], resid_ref.at[part, columns], gone.at[piece, a]).wait()

    inner = inner_ref[0, 0] > 0

    @pl.when(jnp.logical_not(inner))
    def _():
        finish(piece, far_out_ref)
        wait(piece)

    if piece == 0:
        @pl.when(inner)
        def _():
            for i in range(PIECES):
                finish(i, far[i])
            for i in range(PIECES):
                wait(i)


def last_product(total, sums, inner, far, far_out, piece, resid=None, there=()):
    n_own, rows, width = total.shape
    vmem, anywhere = pl.BlockSpec(memory_space=pltpu.VMEM), pl.BlockSpec(memory_space=pl.ANY)
    others = [*there] if resid is None else [resid, *there]
    shape = (rows, n_own * width)
    return pl.pallas_call(
        functools.partial(last_kernel, piece=piece),
        in_specs=[vmem] * (4 + PIECES) + [anywhere] * len(others),
        out_specs=anywhere,
        out_shape=jax.ShapeDtypeStruct(shape, jnp.bfloat16),
        input_output_aliases={} if resid is None else {4 + PIECES: 0},
        scratch_shapes=[
            pltpu.VMEM((PIECES, rows // PIECES, shape[1]), jnp.bfloat16),
            pltpu.SemaphoreType.DMA((PIECES, n_own)),
        ],
        compiler_params=pltpu.CompilerParams(vmem_limit_bytes=16 * MIB),
        cost_estimate=pl.CostEstimate(flops=0, bytes_accessed=1000000, transcendentals=0),
    )(total, sums, inner, *far, far_out, *others)


def dense_local(amplitudes, integrals, cd_tiles, occ_energy, pair_energy):
    rows = amplitudes.shape[0] // lax.axis_size("rep")
    rep_index, vir_index = lax.axis_index("rep"), lax.axis_index("vir")
    swap_near, swap_mid, outward = [(0, 1), (1, 0), (2, 3), (3, 2)], [(1, 2), (2, 1)], [(1, 0), (2, 3)]
    swap_rep = [(0, 1), (1, 0)]

    def send(pieces, pairs):
        return [lax.ppermute(piece, "vir", pairs) for piece in pieces]

    piece = rows // PIECES
    own = [
        lax.dynamic_slice_in_dim(amplitudes, rep_index * rows + i * piece, piece, 0) for i in range(PIECES)
    ]
    vir, rep = vir_index.reshape(1), rep_index.reshape(1)
    occ, pair = occ_energy[None, :], pair_energy[None, :]
    per = amplitudes.shape[1] // integrals.shape[2]
    marks = []

    def after(mark, *held):
        *held, mark = lax.optimization_barrier((*held, mark))
        marks.append(mark)
        return held

    chosen_other = lax.ppermute(cd_tiles, "rep", swap_rep)
    *own, tiles, chosen_other = lax.optimization_barrier((*own, integrals, chosen_other))
    other = lax.ppermute(tiles, "rep", swap_rep)
    near, mid = send(own, swap_near), send(own, swap_mid)
    chosen, mark = near_by(cd_tiles, own[0], chosen_other)
    near[0], = after(mark, near[0])
    n_entry = integrals.shape[1]
    taken, extra = range(n_entry * 8 // 12), range(n_entry * 8 // 12, n_entry)
    mine0, mark, _, _ = tile_sums(vir, chosen, chosen, integrals, 0, taken, None, per, (near[0], mid[0]))
    near[1], mid[1] = after(mark, near[1], mid[1])
    far, mid_out = send(near, swap_mid), send(mid, outward)
    far[0], mid_out[0] = after(all_there(near[1], mid[1]), far[0], mid_out[0])
    mine1, mark, count, entry = tile_sums(
        vir, chosen, chosen_other, integrals, 1, range(n_entry), extra, per, (far[0], mid_out[0])
    )
    mid_out[1], = after(mark, mid_out[1])
    far[1], = after(all_there(mid_out[1]), far[1])
    far_out = send(far, outward)
    total, sums, inner = early_products(
        vir, rep, count, entry, occ, pair, (mine0, mine1), other, integrals, extra, own, near, mid, mid_out
    )
    resid = last_product(total, sums, inner, far, far_out[0], 0, there=marks)
    return last_product(total, sums, inner, far, far_out[1], 1, resid)


def solution(mesh):
    in_specs = (P("occ", "vir"), P("vir", "rep", None, None), P("vir", "rep"), P("occ"), P("vir"))
    out_specs = P(("occ", "rep"), "vir")
    n_rep = mesh.shape["rep"]

    def local(amplitudes, integrals, cd_tiles, occ_energy, pair_energy):
        n_tile = amplitudes.shape[1] * mesh.shape["vir"] // integrals.shape[2]
        few_tiles = n_tile <= n_rep * integrals.shape[1]
        few_tiles &= n_rep == 2 and mesh.shape["vir"] == 4 and integrals.shape[0] == 2 and integrals.shape[1] % 3 == 0
        body = dense_local if few_tiles else sparse_local
        return body(amplitudes, integrals, cd_tiles, occ_energy, pair_energy)

    return jax.shard_map(local, mesh=mesh, in_specs=in_specs, out_specs=out_specs, check_vma=False)
```
